768 devices in a mesh: row: 24 (over z_lo, x), col: 32 (over y, z_hi, core).
Axes of the slice: x: 4, y: 8, z: 12 (z_hi: 2, z_lo: 6; z = z_hi * 6 + z_lo), core: 2. Of those that a mesh axis runs over, the one named last changes fastest.
Arguments:
- values: bfloat16 [24576, 24576], P('row', 'col'), may hold values from -1.5 to 1.5
- pattern: int32 [96, 96], P('row', 'col'), may hold values from 0 to 1, as said below
- sections: int32 [4], replicated, may hold values from 0 to 95
Outputs:
- exposure: bfloat16 [24576, 24576], P('row', 'col')
The draws below stay inside these ranges and needn't reach their ends.
Inputs may be any that keep to these rules, and one draw needn't show every extreme that they name: `pattern`: 1 where a tile is stored, else 0; the share of stored tiles differs from tile row to tile row.
All inputs are finite; a program needn't handle non-finite values.
Results may differ from the reference program's by a relative error of at most 0.001.
Values may be sent and summed in bfloat16 or wider, within the bound.
A program may use at most 64 MiB of HBM per device.

```python
import jax
import jax.numpy as jnp
from jax import lax

TILE = 256
SECTIONS = 4
NT = 96
N = 24576


def draw_pattern(key, part):
    key = jax.random.fold_in(key, 7)
    level_key, roll_key = jax.random.split(key)
    levels = jax.random.randint(level_key, (NT, 1), 0, 4)
    rolls = jax.random.randint(roll_key, (NT, NT), 0, 8)
    return (rolls < 2 + 2 * levels).astype(jnp.int32)


def plant(array, own_key, smallest, high):
    shape = array.shape
    place = [jax.random.randint(jax.random.fold_in(own_key, axis), (), 0, shape[axis]) for axis in range(len(shape))]
    array = array.at[tuple(place)].set(smallest)
    longest = shape.index(max(shape))
    place[longest] = (place[longest] + 1) % shape[longest]
    return array.at[tuple(place)].set(high)


def block_levels(stream_key, dims, cuts, low, largest):
    gain = 1.0
    for position, shards_of in cuts:
        heights = jax.random.uniform(jax.random.fold_in(jax.random.fold_in(stream_key, 6), position), (shards_of,), jnp.float32, low / len(cuts), largest / len(cuts))
        gain = gain * jnp.repeat(jnp.exp(heights), dims[position] // shards_of).reshape((-1,) + (1,) * (len(dims) - 1 - position))
    return gain


def noise(own_key, shape, scale, bound, cuts=(), kind=jnp.bfloat16):
    drawn = jax.random.normal(own_key, shape, jnp.float32) * scale
    if len(cuts) > 0:
        drawn = block_levels(own_key, shape, cuts, -0.22, 0.18) * drawn
    return jnp.clip(drawn, min=-bound, max=bound).astype(kind)


def setup_inputs(seed: int = 0) -> dict:
    streams_of = jax.random.split(jax.random.key(seed), 4)
    return {
        "values": noise(streams_of[0], (N, N), 0.25, 1.5, ((0, 24), (1, 32))),
        "pattern": draw_pattern(jax.random.fold_in(streams_of[3], 71), 0),
        "sections": plant(jax.random.randint(streams_of[2], (SECTIONS,), 0, NT), jax.random.fold_in(streams_of[2], 1), 0, NT - 1).astype(jnp.int32),
    }


def reference(values, pattern, sections):
    flags = pattern.astype(jnp.bfloat16)
    column_list = []
    row_list = []
    for section_number in range(SECTIONS):
        section_index = sections[section_number].astype(jnp.int32)
        column_piece = lax.dynamic_slice_in_dim(values, section_index * TILE, TILE, 1)
        column_flags = lax.dynamic_slice_in_dim(flags, section_index, 1, 1)
        column_piece = column_piece * jnp.repeat(column_flags, TILE, axis=0)
        row_piece = lax.dynamic_slice_in_dim(values, section_index * TILE, TILE, 0)
        row_flags = lax.dynamic_slice_in_dim(flags, section_index, 1, 0)
        row_piece = row_piece * jnp.repeat(row_flags, TILE, axis=1)
        column_list.append(column_piece)
        row_list.append(row_piece)
    left_panels = jnp.concatenate(column_list, axis=1)
    right_panels = jnp.concatenate(row_list, axis=0)

    def tile_row_product(tile_row):
        left_rows = lax.dynamic_slice_in_dim(left_panels, tile_row * TILE, TILE, 0)
        return jnp.dot(left_rows, right_panels, preferred_element_type=jnp.float32).astype(jnp.bfloat16)

    blocks = lax.map(tile_row_product, jnp.arange(NT, dtype=jnp.int32))
    return blocks.reshape(N, N)
```

```python
import jax
import jax.numpy as jnp
from jax import lax
from jax.experimental import pallas as pl
from jax.experimental.pallas import tpu as pltpu
from jax.sharding import PartitionSpec as P

TILE = 256
SECTIONS = 4
X, Y, ZL, ZH, CORES = 4, 8, 6, 2, 2
LB = 64
RB = 64
WIDTH = 768
MESH = pl.DeviceIdType.MESH


def kernel(
    sections, pattern, values, out,
    vals, sib_out, sib_in, own, lrs, zout, zin, left, rown, rrs, rgot, flood, right,
    load_sem, xc_s, xc_r, lrs_s, lrs_r, lz_s, lz_r, lag_s, lag_r, lic_s, lic_r,
    rrs_s, rrs_r, rfl_s, rfl_r, rag_s, rag_r,
):
    row, col = lax.axis_index("row"), lax.axis_index("col")
    x, zl = row % X, row // X
    core, zh, y = col % CORES, col // CORES % ZH, col // (CORES * ZH)
    way = 1 - 2 * core

    def device(dx=0, dy=0, dzl=0, dzh=0, dcore=0):
        r = (zl + dzl) * X + (x + dx + X) % X
        c = ((y + dy + Y) % Y) * (ZH * CORES) + (zh + dzh) % ZH * CORES + (core + dcore) % CORES
        return (r, c)

    def copy(src, dst, send, recv, to):
        return pltpu.make_async_remote_copy(
            src_ref=src, dst_ref=dst, send_sem=send, recv_sem=recv, device_id=to, device_id_type=MESH
        )

    x_fwd, x_back = device(dx=way), device(dx=-way)
    y_fwd, y_back = device(dy=way), device(dy=-way)
    z_far, sibling = device(dzh=1), device(dcore=1)
    z_up, z_down = device(dzl=1), device(dzl=-1)

    load = pltpu.make_async_copy(values, vals, load_sem)
    load.start()
    barrier = pltpu.get_barrier_semaphore()
    for to in (x_fwd, x_back, y_fwd, y_back, z_far, sibling):
        pl.semaphore_signal(barrier, inc=1, device_id=to, device_id_type=MESH)

    @pl.when(zl > 0)
    def _():
        pl.semaphore_signal(barrier, inc=1, device_id=z_down, device_id_type=MESH)

    @pl.when(zl < ZL - 1)
    def _():
        pl.semaphore_signal(barrier, inc=1, device_id=z_up, device_id_type=MESH)

    load.wait()

    def each(body):
        def step(s, carry):
            body(s)
            return carry
        lax.fori_loop(0, SECTIONS, step, 0)

    def lcol(s):
        return sections[s] // 3

    def lroot(s):
        c = lcol(s)
        return c // (CORES * ZH), c // CORES % ZH, c % CORES

    def rroot(s):
        r = sections[s] // 4
        return r % X, r // X

    def factor(condition, scale=1):
        return (condition.astype(jnp.int32) * scale).astype(jnp.float32).astype(jnp.bfloat16)

    def pick(*choices):
        total = None
        for condition, array in choices:
            term = array * factor(condition)
            total = term if total is None else total + term
        return total

    def left_half(half, dst, s):
        lc = sections[s] % 3

        def block(b, carry):
            rows = pl.ds(pl.multiple_of(half * 512 + b * LB, LB), LB)
            total = None
            for k in range(3):
                term = vals[rows, k * TILE : (k + 1) * TILE] * factor(
                    lc == k, pattern[half * 2 + b // 4, k]
                )
                total = term if total is None else total + term
            dst[s, b] = total
            return carry
        lax.fori_loop(0, Y, block, 0)

    def right_piece(s):
        lr = sections[s] % 4
        for k in range(3):
            lanes = slice(k * TILE, (k + 1) * TILE)
            factors = [factor(lr == r, pattern[r, k]) for r in range(4)]

            def block(b, carry):
                total = None
                for r in range(4):
                    rows = pl.ds(pl.multiple_of(r * TILE + b * RB, RB), RB)
                    term = vals[rows, lanes] * factors[r]
                    total = term if total is None else total + term
                rown[s, b, :, lanes] = total
                return carry
            lax.fori_loop(0, X, block, 0)

    def sib_copy(s):
        return copy(sib_out.at[s], sib_in.at[s], xc_s.at[s], xc_r.at[s], sibling)

    each(lambda s: left_half(1 - core, sib_out, s))
    n_z = jnp.where(zl > 0, 1, 0) + jnp.where(zl < ZL - 1, 1, 0)
    pl.semaphore_wait(barrier, 6 + n_z)
    each(lambda s: sib_copy(s).start())

    def rrs_copy(k, s):
        if k == 0:
            src, to = rown.at[s, (x + 2) % X], x_fwd
        elif k == 1:
            src, to = rrs.at[0, s], x_fwd
        else:
            src, to = rown.at[s, (x - way + X) % X], x_back
        return copy(src, rrs.at[k, s], rrs_s.at[k, s], rrs_r.at[k, s], to)

    def right_first(s):
        right_piece(s)
        rrs_copy(0, s).start()
        rrs_copy(2, s).start()
    each(right_first)

    each(lambda s: left_half(core, own, s))

    def lrs_copy(k, s):
        if k < 4:
            src = own.at[s, (y + 4) % Y] if k == 0 else lrs.at[k - 1, s]
            to = y_fwd
        else:
            src = own.at[s, (y - 3 * way + Y) % Y] if k == 4 else lrs.at[k - 1, s]
            to = y_back
        return copy(src, lrs.at[k, s], lrs_s.at[k, s], lrs_r.at[k, s], to)

    def left_first(s):
        sib_copy(s).wait_recv()
        root = lroot(s)[2]
        mine = root == core

        def block(b, carry):
            own[s, b] = pick((mine, own[s, b]), (root != core, sib_in[s, b]))
            return carry
        lax.fori_loop(0, Y, block, 0)
        lrs_copy(0, s).start()
        lrs_copy(4, s).start()
    each(left_first)

    def right_second(s):
        rrs_copy(0, s).wait_recv()
        root = rroot(s)[0]
        rrs[0, s] = pick((root == x, rown[s, (x + way + X) % X]), (root != x, rrs[0, s]))
        rrs_copy(1, s).start()
    each(right_second)

    def left_step(h):
        def body(s):
            root = lroot(s)[0]
            lrs_copy(h - 1, s).wait_recv()
            lrs[h - 1, s] = pick(
                (root == y, own[s, (y + (4 - h) * way + Y) % Y]), (root != y, lrs[h - 1, s])
            )
            lrs_copy(h, s).start()
            if h < 3:
                lrs_copy(3 + h, s).wait_recv()
                lrs[3 + h, s] = pick(
                    (root == y, own[s, (y - (3 - h) * way + Y) % Y]), (root != y, lrs[3 + h, s])
                )
                lrs_copy(4 + h, s).start()
        each(body)

    left_step(1)

    def right_third(s):
        rrs_copy(1, s).wait_recv()
        rrs_copy(2, s).wait_recv()
        delta = ((rroot(s)[0] - x) * way + X) % X
        rgot[s] = pick((delta == 0, rown[s, x]), (delta == 1, rrs[2, s]), (delta >= 2, rrs[1, s]))

    first = zl // 3
    place = jnp.where(first == 0, zl, ZL - 1 - zl)
    second = 1 - first

    def flood_copy(k, s, up):
        return copy(
            flood.at[k, s], flood.at[k, s], rfl_s.at[k, s], rfl_r.at[k, s],
            device(dzl=up),
        )

    def flow_first(at):
        @pl.when(place == at)
        def _():
            def body(s):
                if at == 0:
                    flood[first, s] = rgot[s]
                else:
                    flood_copy(first, s, 1 - 2 * first).wait_recv()
                    root = rroot(s)[1]
                    flood[first, s] = pick((root == zl, rgot[s]), (root != zl, flood[first, s]))
                flood_copy(first, s, 1 - 2 * first).start()
            each(body)

    def rag_copy(k, s):
        block = (x - way + X) % X if k == 1 else x
        to = x_back if k == 2 else x_fwd
        return copy(
            right.at[s, block], right.at[s, block], rag_s.at[k, s], rag_r.at[k, s], to
        )

    def rag_wait(k, s):
        block = [(x - way + X) % X, (x + 2) % X, (x + way + X) % X][k]
        copy(right.at[s, block], right.at[s, block], rag_s.at[k, s], rag_r.at[k, s], x_fwd).wait_recv()

    def flow_second(at):
        @pl.when(place == 5 - at)
        def _():
            def body(s):
                flood_copy(second, s, 2 * first - 1).wait_recv()
                root = rroot(s)[1]
                flood[second, s] = pick((root == zl, rgot[s]), (root != zl, flood[second, s]))
                if at < 5:
                    flood_copy(second, s, 2 * first - 1).start()
                right[s, x] = pick((root <= zl, flood[0, s]), (root > zl, flood[1, s]))
                rag_copy(0, s).start()
                rag_copy(2, s).start()
            each(body)

    def right_last(at):
        @pl.when(place == 5 - at)
        def _():
            def body(s):
                rag_wait(0, s)
                rag_copy(1, s).start()
            each(body)

    each(right_third)
    flow_first(0)
    left_step(2)
    flow_first(1)
    left_step(3)
    flow_first(2)

    def z_copy(s):
        return copy(zout.at[s], zin.at[s], lz_s.at[s], lz_r.at[s], z_far)

    def left_reduced(s):
        lrs_copy(3, s).wait_recv()
        lrs_copy(6, s).wait_recv()
        delta = ((lroot(s)[0] - y) * way + Y) % Y
        near = (delta > 0).astype(jnp.int32) * (delta < 4).astype(jnp.int32)
        zout[s] = pick((delta == 0, own[s, y]), (near == 1, lrs[6, s]), (delta >= 4, lrs[3, s]))
        z_copy(s).start()
    each(left_reduced)

    flow_second(3)
    flow_second(4)

    def lag_copy(k, s):
        block = (y - k * way + Y) % Y if k < 4 else (y + (k - 4) * way + Y) % Y
        place_ = left.at[s, core * Y + block]
        return copy(place_, place_, lag_s.at[k, s], lag_r.at[k, s], y_fwd if k < 4 else y_back)

    def lag_wait(k, s):
        block = (y - (k + 1) * way + 2 * Y) % Y if k < 4 else (y + (k - 3) * way + Y) % Y
        place_ = left.at[s, core * Y + block]
        copy(place_, place_, lag_s.at[k, s], lag_r.at[k, s], y_fwd).wait_recv()

    def block_of(j):
        return (y - j * way + Y) % Y if j < 5 else (y + (j - 4) * way + Y) % Y

    def lic_copy(j, s):
        place_ = left.at[s, core * Y + block_of(j)]
        return copy(place_, place_, lic_s.at[j, s], lic_r.at[j, s], sibling)

    def lic_wait(j, s):
        other = (y + j * way + Y) % Y if j < 5 else (y - (j - 4) * way + Y) % Y
        place_ = left.at[s, (1 - core) * Y + other]
        copy(place_, place_, lic_s.at[j, s], lic_r.at[j, s], sibling).wait_recv()

    def left_gather0(s):
        z_copy(s).wait_recv()
        root = lroot(s)[1]
        left[s, core * Y + y] = pick((root == zh, zout[s]), (root != zh, zin[s]))
        lag_copy(0, s).start()
        lag_copy(4, s).start()
        lic_copy(0, s).start()
    each(left_gather0)

    def left_gather(h):
        def body(s):
            lag_wait(h - 1, s)
            if h < 4:
                lag_copy(h, s).start()
            if h < 4:
                lag_wait(3 + h, s)
                if h < 3:
                    lag_copy(4 + h, s).start()
            lic_copy(h, s).start()
            if h < 4:
                lic_copy(4 + h, s).start()
        each(body)

    left_gather(1)
    flow_second(5)
    right_last(3)
    right_last(4)
    left_gather(2)
    right_last(5)
    left_gather(3)
    left_gather(4)

    def finish(s):
        rag_wait(1, s)
        rag_wait(2, s)
        for j in range(8):
            lic_wait(j, s)
    each(finish)

    def rows_of(i, carry):
        lhs = jnp.concatenate(
            [left[s, pl.ds(4 * i, 4)].reshape(TILE, TILE) for s in range(SECTIONS)], axis=1
        )
        rhs = right[...].reshape(SECTIONS * TILE, WIDTH)
        out[pl.ds(pl.multiple_of(i * TILE, TILE), TILE), :] = jnp.dot(
            lhs, rhs, preferred_element_type=jnp.float32
        ).astype(jnp.bfloat16)
        return carry
    lax.fori_loop(0, 4, rows_of, 0)

    def drain(s):
        sib_copy(s).wait_send()
        z_copy(s).wait_send()
        for k in range(7):
            lrs_copy(k, s).wait_send()
            lag_copy(k, s).wait_send()
        for j in range(8):
            lic_copy(j, s).wait_send()
        for k in range(3):
            rrs_copy(k, s).wait_send()
            rag_copy(k, s).wait_send()
        flood_copy(first, s, 1 - 2 * first).wait_send()

        @pl.when(place > 0)
        def _():
            flood_copy(second, s, 2 * first - 1).wait_send()
    each(drain)


def shards(values, pattern, sections):
    bf = jnp.bfloat16
    S = SECTIONS
    dma = pltpu.SemaphoreType.DMA
    return pl.pallas_call(
        kernel,
        name="exposure",
        out_shape=jax.ShapeDtypeStruct(values.shape, bf),
        in_specs=[
            pl.BlockSpec(memory_space=pltpu.SMEM),
            pl.BlockSpec(memory_space=pltpu.SMEM),
            pl.BlockSpec(memory_space=pl.ANY),
        ],
        out_specs=pl.BlockSpec(memory_space=pltpu.VMEM),
        scratch_shapes=[
            pltpu.VMEM((1024, WIDTH), bf),
            pltpu.VMEM((S, Y, LB, TILE), bf),
            pltpu.VMEM((S, Y, LB, TILE), bf),
            pltpu.VMEM((S, Y, LB, TILE), bf),
            pltpu.VMEM((7, S, LB, TILE), bf),
            pltpu.VMEM((S, LB, TILE), bf),
            pltpu.VMEM((S, LB, TILE), bf),
            pltpu.VMEM((S, 2 * Y, LB, TILE), bf),
            pltpu.VMEM((S, X, RB, WIDTH), bf),
            pltpu.VMEM((3, S, RB, WIDTH), bf),
            pltpu.VMEM((S, RB, WIDTH), bf),
            pltpu.VMEM((2, S, RB, WIDTH), bf),
            pltpu.VMEM((S, X, RB, WIDTH), bf),
            dma,
            dma((S,)), dma((S,)),
            dma((7, S)), dma((7, S)),
            dma((S,)), dma((S,)),
            dma((7, S)), dma((7, S)),
            dma((8, S)), dma((8, S)),
            dma((3, S)), dma((3, S)),
            dma((2, S)), dma((2, S)),
            dma((3, S)), dma((3, S)),
        ],
        compiler_params=pltpu.CompilerParams(
            collective_id=0, has_side_effects=True, vmem_limit_bytes=40 << 20
        ),
        cost_estimate=pl.CostEstimate(
            flops=2 * 1024 * 1024 * 768, bytes_accessed=2 * 1024 * 768 * 2, transcendentals=0
        ),
    )(sections, pattern, values)


def solution(mesh):
    in_specs = (P("row", "col"), P("row", "col"), P())
    out_specs = P("row", "col")
    return jax.shard_map(shards, mesh=mesh, in_specs=in_specs, out_specs=out_specs, check_vma=False)
```

```python
import jax
import jax.numpy as jnp
from jax import lax
from jax.experimental import pallas as pl
from jax.experimental.pallas import tpu as pltpu
from jax.sharding import PartitionSpec as P

TILE = 256
SECTIONS = 4
CHUNKS = 8
X, Y, ZL, ZH, CORES = 4, 8, 6, 2, 2
LB = 64
RB = 64
WIDTH = 768
MESH = pl.DeviceIdType.MESH


XC, LRS, LZ, LAG, LIC, RX, RRS, RFL, RAG, RIC = range(10)


def kernel(
    sections_any, pattern_any, values, out,
    sections, pattern, vals, product,
    sib_out, sib_in, own, lrs, zout, zin, left, ship, rown, rrs, rgot, flood, right,
    load_sems, out_sem, sent, result_r, cross_r, z_r, reduce_r, gather_r,
):
    row, col = lax.axis_index("row"), lax.axis_index("col")
    x, zl = row % X, row // X
    core, zh, y = col % CORES, col // CORES % ZH, col // (CORES * ZH)
    first = zl // 3
    place = (1 - first) * zl + first * (ZL - 1 - zl)
    second = 1 - first

    def device(dx=0, dy=0, dzl=0, dzh=0, dcore=0):
        r = (zl + dzl) * X + (x + dx + X) % X
        c = ((y + dy + Y) % Y) * (ZH * CORES) + (zh + dzh) % ZH * CORES + (core + dcore) % CORES
        return (r, c)

    def copy(src, dst, send, recv, to):
        return pltpu.make_async_remote_copy(
            src_ref=src, dst_ref=dst, send_sem=send, recv_sem=recv, device_id=to, device_id_type=MESH
        )

    def way(q):
        return 1 - 2 * (q % 2)

    sibling = device(dcore=1)
    barrier = pltpu.get_barrier_semaphore()

    def greet(to):
        pl.semaphore_signal(barrier, inc=1, device_id=to, device_id_type=MESH)

    loads = [
        pltpu.make_async_copy(src, dst, load_sems.at[i])
        for i, (src, dst) in enumerate(((values, vals), (sections_any, sections), (pattern_any, pattern)))
    ]
    for load in loads:
        load.start()
    greet(sibling)

    @pl.when(core == 0)
    def _():
        greet(device(dy=1))
        greet(device(dy=-1))
        greet(device(dzh=1))

    @pl.when(core == 1)
    def _():
        greet(device(dx=1))
        greet(device(dx=-1))

        @pl.when(zl > 0)
        def _():
            greet(device(dzl=-1))

        @pl.when(zl < ZL - 1)
        def _():
            greet(device(dzl=1))

    for load in loads:
        load.wait()

    def loop(low, high, body):
        def step(q, carry):
            body(q)
            return carry
        lax.fori_loop(low, high, step, 0)

    def each(body):
        loop(0, CHUNKS, body)

    def lroot(q):
        c = sections[q % SECTIONS] // 3
        return c // (CORES * ZH), c // CORES % ZH, c % CORES

    def rroot(q):
        r = sections[q % SECTIONS] // 4
        return r % X, r // X

    def factor(condition, scale=1):
        return (condition.astype(jnp.int32) * scale).astype(jnp.float32).astype(jnp.bfloat16)

    def pick(*choices):
        total = None
        for condition, array in choices:
            term = array * factor(condition)
            total = term if total is None else total + term
        return total

    def left_piece(dst, q):
        lc = sections[q % SECTIONS] % 3
        half = q // SECTIONS

        def block(b):
            rows = pl.ds(pl.multiple_of(half * 512 + b * LB, LB), LB)
            total = None
            for k in range(3):
                term = vals[rows, k * TILE : (k + 1) * TILE] * factor(
                    lc == k, pattern[half * 2 + b // 4, k]
                )
                total = term if total is None else total + term
            dst[q, b] = total
        loop(0, Y, block)

    def right_piece(dst, s):
        lr = sections[s] % 4
        for k in range(3):
            lanes = slice(k * TILE, (k + 1) * TILE)
            factors = [factor(lr == r, pattern[r, k]) for r in range(4)]

            def block(b):
                total = None
                for r in range(4):
                    rows = pl.ds(pl.multiple_of(r * TILE + b * RB, RB), RB)
                    term = vals[rows, lanes] * factors[r]
                    total = term if total is None else total + term
                dst[s, b, :, lanes] = total
            loop(0, X, block)

    def left_ship(q):
        return copy(sib_out.at[q], sib_in.at[q], sent.at[XC], cross_r.at[q], sibling)

    def right_ship(s):
        return copy(ship.at[s], rown.at[SECTIONS + s], sent.at[RX], cross_r.at[s], sibling)

    def block_of(j, q):
        return (y - j * way(q) + Y) % Y if j < 5 else (y + (j - 4) * way(q) + Y) % Y

    def lic_copy(j, q):
        spot = left.at[q, block_of(j, q)]
        return copy(spot, spot, sent.at[LIC], result_r, sibling)

    def ric_copy(j, q):
        block = (x + [0, -1, 2, 1][j] * way(q) + X) % X
        spot = right.at[q, block]
        return copy(spot, spot, sent.at[RIC], result_r, sibling)

    def lrs_copy(k, q):
        w = way(q)
        if k == 0:
            src = own.at[q, (y + 4) % Y]
        elif k == 4:
            src = own.at[q, (y - 3 * w + Y) % Y]
        else:
            src = lrs.at[k - 1, q]
        to = device(dy=w) if k < 4 else device(dy=-w)
        return copy(src, lrs.at[k, q], sent.at[LRS], reduce_r.at[k, q], to)

    def z_copy(q):
        return copy(zout.at[q], zin.at[q], sent.at[LZ], z_r.at[q], device(dzh=1))

    def lag_copy(k, q):
        w = way(q)
        block = (y - k * w + Y) % Y if k < 4 else (y + (k - 4) * w + Y) % Y
        spot = left.at[q, block]
        to = device(dy=w) if k < 4 else device(dy=-w)
        return copy(spot, spot, sent.at[LAG], gather_r.at[k, q], to)

    def lag_wait(k, q):
        w = way(q)
        block = (y - (k + 1) * w + Y) % Y if k < 4 else (y + (k - 3) * w + Y) % Y
        spot = left.at[q, block]
        copy(spot, spot, sent.at[LAG], gather_r.at[k, q], sibling).wait_recv()

    def rrs_copy(k, q):
        w = way(q)
        if k == 0:
            src = rown.at[q, (x + 2) % X]
        elif k == 1:
            src = rrs.at[0, q]
        else:
            src = rown.at[q, (x - w + X) % X]
        to = device(dx=w) if k < 2 else device(dx=-w)
        return copy(src, rrs.at[k, q], sent.at[RRS], reduce_r.at[k, q], to)

    def flood_copy(k, q):
        spot = flood.at[k, q]
        return copy(spot, spot, sent.at[RFL], reduce_r.at[3 + k, q], device(dzl=1 - 2 * k))

    def rag_copy(k, q):
        w = way(q)
        block = (x - w + X) % X if k == 1 else x
        spot = right.at[q, block]
        to = device(dx=-w) if k == 2 else device(dx=w)
        return copy(spot, spot, sent.at[RAG], gather_r.at[k, q], to)

    def rag_wait(k, q):
        block = (x + [-1, 2, 1][k] * way(q) + X) % X
        spot = right.at[q, block]
        copy(spot, spot, sent.at[RAG], gather_r.at[k, q], sibling).wait_recv()

    def received(ref):
        copy(ref, ref, sent.at[LIC], result_r, sibling).wait_recv()

    def drain(kind, ref):
        copy(ref, ref, sent.at[kind], result_r, sibling).wait_send()

    @pl.when(core == 0)
    def _():
        right_piece(ship, 0)
        pl.semaphore_wait(barrier, 4)

        def begin(s):
            @pl.when(s > 0)
            def _():
                right_piece(ship, s)
            right_ship(s).start()
            left_piece(own, s)
            left_piece(own, s + SECTIONS)
        loop(0, SECTIONS, begin)

        def reduce_first(q):
            left_ship(q).wait_recv()
            root = lroot(q)[2]

            def block(b):
                own[q, b] = pick((root == 0, own[q, b]), (root == 1, sib_in[q, b]))
            loop(0, Y, block)
            lrs_copy(0, q).start()
            lrs_copy(4, q).start()
        each(reduce_first)

        for h in range(1, 4):
            def reduce_next(q, h=h):
                w = way(q)
                root = lroot(q)[0]
                lrs_copy(h - 1, q).wait_recv()
                lrs[h - 1, q] = pick(
                    (root == y, own[q, (y + (4 - h) * w + Y) % Y]), (root != y, lrs[h - 1, q])
                )
                lrs_copy(h, q).start()
                if h < 3:
                    lrs_copy(3 + h, q).wait_recv()
                    lrs[3 + h, q] = pick(
                        (root == y, own[q, (y - (3 - h) * w + Y) % Y]), (root != y, lrs[3 + h, q])
                    )
                    lrs_copy(4 + h, q).start()
            each(reduce_next)

        def reduce_last(q):
            lrs_copy(3, q).wait_recv()
            lrs_copy(6, q).wait_recv()
            delta = ((lroot(q)[0] - y) * way(q) + Y) % Y
            near = (delta > 0).astype(jnp.int32) * (delta < 4).astype(jnp.int32)
            zout[q] = pick((delta == 0, own[q, y]), (near == 1, lrs[6, q]), (delta >= 4, lrs[3, q]))
            z_copy(q).start()
        each(reduce_last)

        def gather_first(q):
            z_copy(q).wait_recv()
            root = lroot(q)[1]
            left[q, y] = pick((root == zh, zout[q]), (root != zh, zin[q]))
            lag_copy(0, q).start()
            lag_copy(4, q).start()
            lic_copy(0, q).start()
        each(gather_first)

        for h in range(1, 5):
            def gather_next(q, h=h):
                lag_wait(h - 1, q)
                if h < 4:
                    lag_copy(h, q).start()
                    lag_wait(3 + h, q)
                    if h < 3:
                        lag_copy(4 + h, q).start()
                    lic_copy(4 + h, q).start()
                lic_copy(h, q).start()
            each(gather_next)

        received(right.at[pl.ds(SECTIONS, SECTIONS)])

    @pl.when(core == 1)
    def _():
        left_piece(sib_out, 0)
        up = (zl > 0).astype(jnp.int32) + (zl < ZL - 1).astype(jnp.int32)
        pl.semaphore_wait(barrier, 3 + up)

        def begin(s):
            @pl.when(s > 0)
            def _():
                left_piece(sib_out, s)
            left_ship(s).start()
            right_piece(rown, s)
            rrs_copy(0, s).start()
            left_piece(sib_out, s + SECTIONS)
            left_ship(s + SECTIONS).start()
        loop(0, SECTIONS, begin)

        def shipped(s):
            right_ship(s).wait_recv()
            rrs_copy(0, s + SECTIONS).start()
        loop(0, SECTIONS, shipped)

        def reduce_next(q):
            root = rroot(q)[0]
            rrs_copy(0, q).wait_recv()
            rrs[0, q] = pick((root == x, rown[q, (x + way(q) + X) % X]), (root != x, rrs[0, q]))
            rrs_copy(1, q).start()
            rrs_copy(2, q).start()

        def reduce_last(q):
            rrs_copy(1, q).wait_recv()
            rrs_copy(2, q).wait_recv()
            delta = ((rroot(q)[0] - x) * way(q) + X) % X
            rgot[q] = pick((delta == 0, rown[q, x]), (delta == 1, rrs[2, q]), (delta >= 2, rrs[1, q]))

        def flow_first(q):
            @pl.when(place == 0)
            def _():
                flood[first, q] = rgot[q]

            @pl.when(place > 0)
            def _():
                flood_copy(first, q).wait_recv()
                root = rroot(q)[1]
                flood[first, q] = pick((root == zl, rgot[q]), (root != zl, flood[first, q]))
            flood_copy(first, q).start()

        def flow_second(q):
            flood_copy(second, q).wait_recv()
            root = rroot(q)[1]
            flood[second, q] = pick((root == zl, rgot[q]), (root != zl, flood[second, q]))

            @pl.when(place > 0)
            def _():
                flood_copy(second, q).start()
            right[q, x] = pick((root <= zl, flood[0, q]), (root > zl, flood[1, q]))
            rag_copy(0, q).start()
            rag_copy(2, q).start()

            @pl.when(q >= SECTIONS)
            def _():
                ric_copy(0, q).start()

        def gather_next(q):
            rag_wait(0, q)
            rag_copy(1, q).start()

            @pl.when(q >= SECTIONS)
            def _():
                ric_copy(1, q).start()

        def gather_last(q):
            rag_wait(2, q)

            @pl.when(q >= SECTIONS)
            def _():
                ric_copy(3, q).start()
            rag_wait(1, q)

            @pl.when(q >= SECTIONS)
            def _():
                ric_copy(2, q).start()

        lag_first = 3 + (5 * place + 1) // 2
        lag_second = 3 + (5 * (5 - place) + 1) // 2

        def step(t):
            for lag, body in (
                (0, reduce_next),
                (3, reduce_last),
                (lag_first, flow_first),
                (lag_second, flow_second),
                (lag_second + 3, gather_next),
                (lag_second + 6, gather_last),
            ):
                @pl.when((t >= lag) & (t < lag + CHUNKS))
                def _(body=body, lag=lag):
                    body(t - lag)
        loop(0, CHUNKS + 22, step)

        received(left)

    def rows_of(i):
        lhs = jnp.concatenate(
            [
                left[i // 2 * SECTIONS + s, pl.ds(i % 2 * 4, 4)].reshape(TILE, TILE)
                for s in range(SECTIONS)
            ],
            axis=1,
        )
        rhs = right[pl.ds((1 - core) * SECTIONS, SECTIONS)].reshape(SECTIONS * TILE, WIDTH)
        rows = pl.ds(pl.multiple_of(i * TILE, TILE), TILE)
        product[rows, :] = jnp.dot(lhs, rhs, preferred_element_type=jnp.float32).astype(jnp.bfloat16)
        pltpu.make_async_copy(product.at[rows], out.at[rows], out_sem).start()
    loop(0, 4, rows_of)

    @pl.when(core == 0)
    def _():
        drain(RX, ship)
        drain(LRS, lrs)
        drain(LZ, zout)
        drain(LAG, left.at[:, pl.ds(0, 7)])
        drain(LIC, left)

    @pl.when(core == 1)
    def _():
        drain(XC, sib_out)
        drain(RRS, rrs)
        drain(RFL, flood.at[first])

        @pl.when(place > 0)
        def _():
            drain(RFL, flood.at[second])
        drain(RAG, right.at[:, pl.ds(0, 3)])
        drain(RIC, right.at[pl.ds(SECTIONS, SECTIONS)])

    pltpu.make_async_copy(product, out, out_sem).wait()


def shards(values, pattern, sections):
    bf = jnp.bfloat16
    S, C = SECTIONS, CHUNKS
    dma = pltpu.SemaphoreType.DMA
    return pl.pallas_call(
        kernel,
        name="exposure",
        out_shape=jax.ShapeDtypeStruct(values.shape, bf),
        in_specs=[
            pl.BlockSpec(memory_space=pl.ANY),
            pl.BlockSpec(memory_space=pl.ANY),
            pl.BlockSpec(memory_space=pl.ANY),
        ],
        out_specs=pl.BlockSpec(memory_space=pl.ANY),
        scratch_shapes=[
            pltpu.SMEM((S,), jnp.int32),
            pltpu.SMEM((4, 3), jnp.int32),
            pltpu.VMEM((1024, WIDTH), bf),
            pltpu.VMEM((1024, WIDTH), bf),
            pltpu.VMEM((C, Y, LB, TILE), bf),
            pltpu.VMEM((C, Y, LB, TILE), bf),
            pltpu.VMEM((C, Y, LB, TILE), bf),
            pltpu.VMEM((7, C, LB, TILE), bf),
            pltpu.VMEM((C, LB, TILE), bf),
            pltpu.VMEM((C, LB, TILE), bf),
            pltpu.VMEM((C, Y, LB, TILE), bf),
            pltpu.VMEM((S, X, RB, WIDTH), bf),
            pltpu.VMEM((C, X, RB, WIDTH), bf),
            pltpu.VMEM((3, C, RB, WIDTH), bf),
            pltpu.VMEM((C, RB, WIDTH), bf),
            pltpu.VMEM((2, C, RB, WIDTH), bf),
            pltpu.VMEM((C, X, RB, WIDTH), bf),
            dma((3,)), dma, dma((10,)), dma, dma((C,)), dma((C,)), dma((7, C)), dma((7, C)),
        ],
        compiler_params=pltpu.CompilerParams(
            collective_id=0, has_side_effects=True, vmem_limit_bytes=60 << 20
        ),
        cost_estimate=pl.CostEstimate(
            flops=2 * 1024 * 1024 * 768, bytes_accessed=2 * 1024 * 768 * 2, transcendentals=0
        ),
    )(sections, pattern, values)


def solution(mesh):
    in_specs = (P("row", "col"), P("row", "col"), P())
    out_specs = P("row", "col")
    return jax.shard_map(shards, mesh=mesh, in_specs=in_specs, out_specs=out_specs, check_vma=False)
```

```python
import jax
import jax.numpy as jnp
from jax import lax
from jax.experimental import pallas as pl
from jax.experimental.pallas import tpu as pltpu
from jax.sharding import PartitionSpec as P

TILE = 256
SECTIONS = 4
CHUNKS = 8
PIECES = 16
X, Y, ZL, ZH, CORES = 4, 8, 6, 2, 2
LB = 64
ORDER = (4, 3, -3, 2, -2, 1, -1, 0)
RB = 32
WIDTH = 768
MESH = pl.DeviceIdType.MESH


XC, LRS, LZ, LAG, LIC, RX, RRS, RFL, RAG, RIC = range(10)


def kernel(
    sections_any, pattern_any, values, out,
    sections, pattern, table, pieces, vals, product,
    sib_out, sib_in, own, lrs, zout, zin, left, ship, rown, rrs, rgot, flood, right,
    load_sems, out_sem, sent, result_r, cross_r, z_r, reduce_r, gather_r, along_r,
):
    row, col = lax.axis_index("row"), lax.axis_index("col")
    x, zl = row % X, row // X
    core, zh, y = col % CORES, col // CORES % ZH, col // (CORES * ZH)
    first = zl // 3
    place = (1 - first) * zl + first * (ZL - 1 - zl)
    second = 1 - first

    def device(dx=0, dy=0, dzl=0, dzh=0, dcore=0):
        r = (zl + dzl) * X + (x + dx + X) % X
        c = ((y + dy + Y) % Y) * (ZH * CORES) + (zh + dzh) % ZH * CORES + (core + dcore) % CORES
        return (r, c)

    def copy(src, dst, send, recv, to):
        return pltpu.make_async_remote_copy(
            src_ref=src, dst_ref=dst, send_sem=send, recv_sem=recv, device_id=to, device_id_type=MESH
        )

    on_y = {d: device(dy=d) for d in (-1, 1)}
    on_x = {d: device(dx=d) for d in (-1, 1)}
    z_far = device(dzh=1)
    yb = {d: (y + d + Y) % Y for d in range(-4, 5)}
    xb = {d: (x + d + X) % X for d in range(-2, 3)}

    class Chunk:
        def __init__(self, index, way):
            self.index, self.way = index, way

    sibling = device(dcore=1)
    barrier = pltpu.get_barrier_semaphore()

    def greet(to):
        pl.semaphore_signal(barrier, inc=1, device_id=to, device_id_type=MESH)

    loads = [
        pltpu.make_async_copy(src, dst, load_sems.at[i])
        for i, (src, dst) in enumerate(((values, vals), (sections_any, sections), (pattern_any, pattern)))
    ]
    for load in loads:
        load.start()
    greet(sibling)

    @pl.when(core == 0)
    def _():
        greet(on_y[1])
        greet(on_y[-1])
        greet(z_far)

    @pl.when(core == 1)
    def _():
        greet(on_x[1])
        greet(on_x[-1])

        @pl.when(zl > 0)
        def _():
            greet(device(dzl=-1))

        @pl.when(zl < ZL - 1)
        def _():
            greet(device(dzl=1))

    for load in loads:
        load.wait()

    def loop(low, high, body):
        def step(q, carry):
            body(q)
            return carry
        lax.fori_loop(low, high, step, 0)

    def each(body, low=0, high=CHUNKS):
        def pair(i):
            for parity in range(2):
                body(Chunk(2 * i + parity, 1 - 2 * parity))
        loop(low // 2, high // 2, pair)

    def tabulate(s):
        c, r = sections[s] // 3, sections[s] // 4
        entries = (c // (CORES * ZH), c // CORES % ZH, c % CORES, r % X, r // X)
        for i, entry in enumerate(entries):
            table[i, s] = entry
            table[i, s + SECTIONS] = entry
            pieces[i, 2 * s] = entry
            pieces[i, 2 * s + 1] = entry
            pieces[i, 2 * s + CHUNKS] = entry
            pieces[i, 2 * s + 1 + CHUNKS] = entry
    loop(0, SECTIONS, tabulate)

    def factor(condition, scale=1):
        return (condition.astype(jnp.int32) * scale).astype(jnp.float32).astype(jnp.bfloat16)

    def pick(*choices):
        total = None
        for condition, array in choices:
            term = array * factor(condition)
            total = term if total is None else total + term
        return total

    def left_block(dst, d):
        b = yb[d]

        def chunk(q):
            lc = sections[q % SECTIONS] % 3
            half = q // SECTIONS
            rows = pl.ds(pl.multiple_of(half * 512 + b * LB, LB), LB)
            total = None
            for k in range(3):
                term = vals[rows, k * TILE : (k + 1) * TILE] * factor(
                    lc == k, pattern[half * 2 + b // 4, k]
                )
                total = term if total is None else total + term
            dst[b, q] = total
        loop(0, CHUNKS, chunk)

    def right_piece(dst, q):
        s, half = q // 2, q % 2
        lr = sections[s] % 4
        for k in range(3):
            lanes = slice(k * TILE, (k + 1) * TILE)
            factors = [factor(lr == r, pattern[r, k]) for r in range(4)]

            def block(b):
                total = None
                for r in range(4):
                    start = r * TILE + half * (TILE // 2) + b * RB
                    term = vals[pl.ds(pl.multiple_of(start, RB), RB), lanes] * factors[r]
                    total = term if total is None else total + term
                dst[q, b, :, lanes] = total
            loop(0, X, block)

    def left_ship(d):
        b, i = yb[d], ORDER.index(d)
        return copy(sib_out.at[b], sib_in.at[b], sent.at[XC], cross_r.at[i], sibling)

    def right_ship(s):
        return copy(ship.at[s], rown.at[CHUNKS + s], sent.at[RX], cross_r.at[s], sibling)

    def block_of(j, w):
        return yb[-j * w] if j < 5 else yb[(j - 4) * w]

    def lic_copy(j, chunk):
        spot = left.at[chunk.index, block_of(j, chunk.way)]
        return copy(spot, spot, sent.at[LIC], result_r.at[chunk.index // SECTIONS], sibling)

    def ric_copy(j, chunk):
        spot = right.at[chunk.index, xb[(0, -1, 2, 1)[j] * chunk.way]]
        return copy(spot, spot, sent.at[RIC], result_r.at[0], sibling)

    def lrs_copy(k, chunk):
        q, w = chunk.index, chunk.way
        if k == 0:
            src = own.at[yb[4], q]
        elif k == 4:
            src = own.at[yb[-3 * w], q]
        else:
            src = lrs.at[k - 1, q]
        to = on_y[w] if k < 4 else on_y[-w]
        return copy(src, lrs.at[k, q], sent.at[LRS], reduce_r.at[k, q], to)

    def z_copy(chunk):
        q = chunk.index
        return copy(zout.at[q], zin.at[q], sent.at[LZ], z_r.at[q], z_far)

    def lag_copy(k, chunk):
        q, w = chunk.index, chunk.way
        spot = left.at[q, yb[-k * w] if k < 4 else yb[(k - 4) * w]]
        to = on_y[w] if k < 4 else on_y[-w]
        return copy(spot, spot, sent.at[LAG], gather_r.at[k, q], to)

    def lag_wait(k, chunk):
        q, w = chunk.index, chunk.way
        spot = left.at[q, yb[-(k + 1) * w] if k < 4 else yb[(k - 3) * w]]
        copy(spot, spot, sent.at[LAG], gather_r.at[k, q], sibling).wait_recv()

    def rrs_copy(k, chunk):
        q, w = chunk.index, chunk.way
        if k == 0:
            src = rown.at[q, xb[2]]
        elif k == 1:
            src = rrs.at[0, q]
        else:
            src = rown.at[q, xb[-w]]
        to = on_x[w] if k < 2 else on_x[-w]
        return copy(src, rrs.at[k, q], sent.at[RRS], along_r.at[k, q], to)

    first_to = device(dzl=1 - 2 * first)
    second_to = device(dzl=2 * first - 1)

    def flood_copy(k, chunk):
        q = chunk.index
        spot = flood.at[k, q]
        to = first_to if k is first else second_to
        return copy(spot, spot, sent.at[RFL], along_r.at[3 + k, q], to)

    def rag_copy(k, chunk):
        q, w = chunk.index, chunk.way
        spot = right.at[q, xb[-w] if k == 1 else x]
        to = on_x[-w] if k == 2 else on_x[w]
        return copy(spot, spot, sent.at[RAG], along_r.at[5 + k, q], to)

    def rag_wait(k, chunk):
        q, w = chunk.index, chunk.way
        spot = right.at[q, xb[(-1, 2, 1)[k] * w]]
        copy(spot, spot, sent.at[RAG], along_r.at[5 + k, q], sibling).wait_recv()

    def received(part, ref):
        copy(ref, ref, sent.at[LIC], result_r.at[part], sibling).wait_recv()

    def drain(kind, ref):
        copy(ref, ref, sent.at[kind], result_r.at[0], sibling).wait_send()

    @pl.when(core == 0)
    def _():
        for d in ORDER[:3]:
            left_block(own, d)
        pl.semaphore_wait(barrier, 4)
        for d in ORDER[:3]:
            left_ship(d).wait_recv()

        def reduce_first(chunk):
            q = chunk.index
            here, there = factor(table[2, q] == 0), factor(table[2, q] == 1)
            for k, d in ((0, 4), (4, -3 * chunk.way)):
                own[yb[d], q] = own[yb[d], q] * here + sib_in[yb[d], q] * there
                lrs_copy(k, chunk).start()
        each(reduce_first)

        def begin(s):
            right_piece(ship, s)
            right_ship(s).start()
        loop(0, CHUNKS, begin)
        for d in ORDER[3:]:
            left_block(own, d)

        def merge(q, d, got):
            mine = (table[0, q] == y).astype(jnp.int32)
            here, there = factor(table[2, q] == 0, mine), factor(table[2, q] == 1, mine)
            return own[yb[d], q] * here + sib_in[yb[d], q] * there + got * factor(mine == 0)

        for h in range(1, 4):
            if h < 3:
                left_ship(3 - h).wait_recv()
                left_ship(h - 3).wait_recv()

            def reduce_next(chunk, h=h):
                q, w = chunk.index, chunk.way
                lrs_copy(h - 1, chunk).wait_recv()
                lrs[h - 1, q] = merge(q, (4 - h) * w, lrs[h - 1, q])
                lrs_copy(h, chunk).start()
                if h < 3:
                    lrs_copy(3 + h, chunk).wait_recv()
                    lrs[3 + h, q] = merge(q, -(3 - h) * w, lrs[3 + h, q])
                    lrs_copy(4 + h, chunk).start()
            each(reduce_next)
        left_ship(0).wait_recv()

        def reduce_last(chunk):
            q, w = chunk.index, chunk.way
            delta = ((table[0, q] - y) * w + Y) % Y
            near = (delta > 0).astype(jnp.int32) * (delta < 4).astype(jnp.int32)
            lrs_copy(6, chunk).wait_recv()
            lrs_copy(3, chunk).wait_recv()
            far = lrs[6, q] * factor(near == 1) + lrs[3, q] * factor(delta >= 4)
            zout[q] = merge(q, 0, far)
            z_copy(chunk).start()
        each(reduce_last)

        def gather_first(chunk):
            q = chunk.index
            root = table[1, q]
            mine, other = factor(root == zh), factor(root != zh)
            z_copy(chunk).wait_recv()
            left[q, y] = zout[q] * mine + zin[q] * other
            lag_copy(0, chunk).start()
            lag_copy(4, chunk).start()
            lic_copy(0, chunk).start()
        each(gather_first)

        for h in range(1, 5):
            def gather_next(chunk, h=h):
                lag_wait(h - 1, chunk)
                if h < 4:
                    lag_copy(h, chunk).start()
                    lag_wait(3 + h, chunk)
                    if h < 3:
                        lag_copy(4 + h, chunk).start()
                    lic_copy(4 + h, chunk).start()
                lic_copy(h, chunk).start()
            each(gather_next)

        received(0, right.at[pl.ds(CHUNKS, CHUNKS)])

    @pl.when(core == 1)
    def _():
        left_block(sib_out, ORDER[0])
        up = (zl > 0).astype(jnp.int32) + (zl < ZL - 1).astype(jnp.int32)
        pl.semaphore_wait(barrier, 3 + up)

        for i, d in enumerate(ORDER):
            if i > 0:
                left_block(sib_out, d)
            left_ship(d).start()
            if i < 2:
                continue
            for q in ((0, 1), (2, 3), (4,), (5,), (6,), (7,))[i - 2]:
                right_piece(rown, q)
                rrs_copy(0, Chunk(q, 1 - 2 * (q % 2))).start()

        def shipped(chunk):
            right_ship(chunk.index - CHUNKS).wait_recv()
            rrs_copy(0, chunk).start()
        each(shipped, CHUNKS, PIECES)

        def reduce_next(chunk):
            q, w = chunk.index, chunk.way
            root = pieces[3, q]
            mine, other = factor(root == x), factor(root != x)
            rrs_copy(0, chunk).wait_recv()
            rrs[0, q] = rown[q, xb[w]] * mine + rrs[0, q] * other
            rrs_copy(1, chunk).start()
            rrs_copy(2, chunk).start()

        def reduce_last(chunk):
            q = chunk.index
            delta = ((pieces[3, q] - x) * chunk.way + X) % X
            rrs_copy(2, chunk).wait_recv()
            rrs_copy(1, chunk).wait_recv()
            rgot[q] = pick((delta == 0, rown[q, x]), (delta == 1, rrs[2, q]), (delta >= 2, rrs[1, q]))

        def flow_first(chunk):
            q = chunk.index

            @pl.when(place == 0)
            def _():
                flood[first, q] = rgot[q]

            @pl.when(place > 0)
            def _():
                root = pieces[4, q]
                mine, other = factor(root == zl), factor(root != zl)
                flood_copy(first, chunk).wait_recv()
                flood[first, q] = rgot[q] * mine + flood[first, q] * other
            flood_copy(first, chunk).start()

        def flow_second(chunk):
            q = chunk.index
            root = pieces[4, q]
            mine, other = factor(root == zl), factor(root != zl)
            flood_copy(second, chunk).wait_recv()
            flood[second, q] = rgot[q] * mine + flood[second, q] * other

            @pl.when(place > 0)
            def _():
                flood_copy(second, chunk).start()
            right[q, x] = pick((root <= zl, flood[0, q]), (root > zl, flood[1, q]))
            rag_copy(0, chunk).start()
            rag_copy(2, chunk).start()

            @pl.when(q >= CHUNKS)
            def _():
                ric_copy(0, chunk).start()

        def gather_next(chunk):
            rag_wait(0, chunk)
            rag_copy(1, chunk).start()

            @pl.when(chunk.index >= CHUNKS)
            def _():
                ric_copy(1, chunk).start()

        def gather_last(chunk):
            rag_wait(2, chunk)
            rag_wait(1, chunk)

            @pl.when(chunk.index >= CHUNKS)
            def _():
                ric_copy(3, chunk).start()
                ric_copy(2, chunk).start()

        lag_first = 8 + 4 * place
        lag_second = 8 + 4 * (5 - place)

        def step(u):
            for parity in range(2):
                t = 2 * u + parity
                for lag, body in (
                    (0, reduce_next),
                    (8, reduce_last),
                    (lag_first, flow_first),
                    (lag_second, flow_second),
                    (lag_second + 8, gather_next),
                    (lag_second + 16, gather_last),
                ):
                    @pl.when((t >= lag) & (t < lag + PIECES))
                    def _(body=body, lag=lag, t=t, parity=parity):
                        body(Chunk(t - lag, 1 - 2 * parity))
        loop(0, (PIECES + 44) // 2, step)


    def rows_of(i):
        lhs = jnp.concatenate(
            [
                left[i // 2 * SECTIONS + s, pl.ds(i % 2 * 4, 4)].reshape(TILE, TILE)
                for s in range(SECTIONS)
            ],
            axis=1,
        )
        rhs = right[pl.ds((1 - core) * CHUNKS, CHUNKS)].reshape(SECTIONS * TILE, WIDTH)
        rows = pl.ds(pl.multiple_of(i * TILE, TILE), TILE)
        product[rows, :] = jnp.dot(lhs, rhs, preferred_element_type=jnp.float32).astype(jnp.bfloat16)
        pltpu.make_async_copy(product.at[rows], out.at[rows], out_sem).start()
    for half in range(2):
        @pl.when(core == 1)
        def _(half=half):
            received(half, left.at[pl.ds(half * SECTIONS, SECTIONS)])
        loop(2 * half, 2 * half + 2, rows_of)

    @pl.when(core == 0)
    def _():
        drain(RX, ship)
        drain(LRS, lrs)
        drain(LZ, zout)
        drain(LAG, left.at[:, pl.ds(0, 7)])
        drain(LIC, left)

    @pl.when(core == 1)
    def _():
        drain(XC, sib_out)
        drain(RRS, rrs)
        drain(RFL, flood.at[first])

        @pl.when(place > 0)
        def _():
            drain(RFL, flood.at[second])
        drain(RAG, right.at[:, pl.ds(0, 3)])
        drain(RIC, right.at[pl.ds(CHUNKS, CHUNKS)])

    pltpu.make_async_copy(product, out, out_sem).wait()


def shards(values, pattern, sections):
    bf = jnp.bfloat16
    S, C = SECTIONS, CHUNKS
    dma = pltpu.SemaphoreType.DMA
    return pl.pallas_call(
        kernel,
        name="exposure",
        out_shape=jax.ShapeDtypeStruct(values.shape, bf),
        in_specs=[
            pl.BlockSpec(memory_space=pl.ANY),
            pl.BlockSpec(memory_space=pl.ANY),
            pl.BlockSpec(memory_space=pl.ANY),
        ],
        out_specs=pl.BlockSpec(memory_space=pl.ANY),
        scratch_shapes=[
            pltpu.SMEM((S,), jnp.int32),
            pltpu.SMEM((4, 3), jnp.int32),
            pltpu.SMEM((5, C), jnp.int32),
            pltpu.SMEM((5, PIECES), jnp.int32),
            pltpu.VMEM((1024, WIDTH), bf),
            pltpu.VMEM((1024, WIDTH), bf),
            pltpu.VMEM((Y, C, LB, TILE), bf),
            pltpu.VMEM((Y, C, LB, TILE), bf),
            pltpu.VMEM((Y, C, LB, TILE), bf),
            pltpu.VMEM((7, C, LB, TILE), bf),
            pltpu.VMEM((C, LB, TILE), bf),
            pltpu.VMEM((C, LB, TILE), bf),
            pltpu.VMEM((C, Y, LB, TILE), bf),
            pltpu.VMEM((C, X, RB, WIDTH), bf),
            pltpu.VMEM((PIECES, X, RB, WIDTH), bf),
            pltpu.VMEM((3, PIECES, RB, WIDTH), bf),
            pltpu.VMEM((PIECES, RB, WIDTH), bf),
            pltpu.VMEM((2, PIECES, RB, WIDTH), bf),
            pltpu.VMEM((PIECES, X, RB, WIDTH), bf),
            dma((3,)), dma, dma((10,)), dma((2,)), dma((C,)), dma((C,)), dma((7, C)), dma((7, C)),
            dma((8, PIECES)),
        ],
        compiler_params=pltpu.CompilerParams(
            collective_id=0, has_side_effects=True, vmem_limit_bytes=60 << 20
        ),
        cost_estimate=pl.CostEstimate(
            flops=2 * 1024 * 1024 * 768, bytes_accessed=2 * 1024 * 768 * 2, transcendentals=0
        ),
    )(sections, pattern, values)


def solution(mesh):
    in_specs = (P("row", "col"), P("row", "col"), P())
    out_specs = P("row", "col")
    return jax.shard_map(shards, mesh=mesh, in_specs=in_specs, out_specs=out_specs, check_vma=False)
```

```python
import jax
import jax.numpy as jnp
from jax import lax
from jax.experimental import pallas as pl
from jax.experimental.pallas import tpu as pltpu
from jax.sharding import PartitionSpec as P

TILE = 256
SECTIONS = 4
CHUNKS = 8
PIECES = 16
X, Y, ZL, ZH, CORES = 4, 8, 6, 2, 2
LB = 64
ORDER = (4, 3, -3, 2, -2, 1, -1, 0)
RB = 32
WIDTH = 768
MESH = pl.DeviceIdType.MESH


XC, LRS, LZ, LAG, LIC, RX, RRS, RFL, RAG, RIC = range(10)


def kernel(
    sections_any, pattern_any, values, out,
    sections, pattern, table, pieces, vals, product,
    sib_out, sib_in, own, lrs, zout, zin, left, ship, rown, rrs, rgot, flood, right,
    load_sems, out_sem, sent, result_r, cross_r, z_r, along_r,
):
    row, col = lax.axis_index("row"), lax.axis_index("col")
    x, zl = row % X, row // X
    core, zh, y = col % CORES, col // CORES % ZH, col // (CORES * ZH)
    first = zl // 3
    place = (1 - first) * zl + first * (ZL - 1 - zl)
    second = 1 - first

    def device(dx=0, dy=0, dzl=0, dzh=0, dcore=0):
        r = (zl + dzl) * X + (x + dx + X) % X
        c = ((y + dy + Y) % Y) * (ZH * CORES) + (zh + dzh) % ZH * CORES + (core + dcore) % CORES
        return (r, c)

    def copy(src, dst, send, recv, to):
        return pltpu.make_async_remote_copy(
            src_ref=src, dst_ref=dst, send_sem=send, recv_sem=recv, device_id=to, device_id_type=MESH
        )

    on_y = {d: device(dy=d) for d in (-1, 1)}
    on_x = {d: device(dx=d) for d in (-1, 1)}
    z_far = device(dzh=1)
    yb = {d: (y + d + Y) % Y for d in range(-4, 5)}
    xb = {d: (x + d + X) % X for d in range(-2, 3)}

    class Chunk:
        def __init__(self, index, way):
            self.index, self.way = index, way

    sibling = device(dcore=1)
    barrier = pltpu.get_barrier_semaphore()

    def greet(to):
        pl.semaphore_signal(barrier, inc=1, device_id=to, device_id_type=MESH)

    loads = [
        pltpu.make_async_copy(src, dst, load_sems.at[i])
        for i, (src, dst) in enumerate(((values, vals), (sections_any, sections), (pattern_any, pattern)))
    ]
    for load in loads:
        load.start()
    greet(sibling)

    @pl.when(core == 0)
    def _():
        greet(on_y[1])
        greet(on_y[-1])
        greet(z_far)

    @pl.when(core == 1)
    def _():
        greet(on_x[1])
        greet(on_x[-1])

        @pl.when(zl > 0)
        def _():
            greet(device(dzl=-1))

        @pl.when(zl < ZL - 1)
        def _():
            greet(device(dzl=1))

    for load in loads:
        load.wait()

    def loop(low, high, body):
        def step(q, carry):
            body(q)
            return carry
        lax.fori_loop(low, high, step, 0)

    def each(body, low=0, high=CHUNKS):
        def pair(i):
            for parity in range(2):
                body(Chunk(2 * i + parity, 1 - 2 * parity))
        loop(low // 2, high // 2, pair)

    def tabulate(s):
        c, r = sections[s] // 3, sections[s] // 4
        entries = (c // (CORES * ZH), c // CORES % ZH, c % CORES, r % X, r // X)
        for i, entry in enumerate(entries):
            table[i, s] = entry
            table[i, s + SECTIONS] = entry
            pieces[i, 2 * s] = entry
            pieces[i, 2 * s + 1] = entry
            pieces[i, 2 * s + CHUNKS] = entry
            pieces[i, 2 * s + 1 + CHUNKS] = entry
    loop(0, SECTIONS, tabulate)

    def factor(condition, scale=1):
        return (condition.astype(jnp.int32) * scale).astype(jnp.float32).astype(jnp.bfloat16)

    def pick(*choices):
        total = None
        for condition, array in choices:
            term = array * factor(condition)
            total = term if total is None else total + term
        return total

    def left_block(dst, d):
        b = yb[d]

        def chunk(q):
            lc = sections[q % SECTIONS] % 3
            half = q // SECTIONS
            rows = pl.ds(pl.multiple_of(half * 512 + b * LB, LB), LB)
            total = None
            for k in range(3):
                term = vals[rows, k * TILE : (k + 1) * TILE] * factor(
                    lc == k, pattern[half * 2 + b // 4, k]
                )
                total = term if total is None else total + term
            dst[b, q] = total
        loop(0, CHUNKS, chunk)

    def right_piece(dst, q):
        s, half = q // 2, q % 2
        lr = sections[s] % 4
        for k in range(3):
            lanes = slice(k * TILE, (k + 1) * TILE)
            factors = [factor(lr == r, pattern[r, k]) for r in range(4)]

            def block(b):
                total = None
                for r in range(4):
                    start = r * TILE + half * (TILE // 2) + b * RB
                    term = vals[pl.ds(pl.multiple_of(start, RB), RB), lanes] * factors[r]
                    total = term if total is None else total + term
                dst[q, b, :, lanes] = total
            loop(0, X, block)

    def left_ship(d):
        b, i = yb[d], ORDER.index(d)
        return copy(sib_out.at[b], sib_in.at[b], sent.at[XC], cross_r.at[i], sibling)

    def right_ship(s):
        return copy(ship.at[s], rown.at[CHUNKS + s], sent.at[RX], cross_r.at[s], sibling)

    def block_of(j, w):
        return yb[-j * w] if j < 5 else yb[(j - 4) * w]

    def lic_copy(j, chunk):
        spot = left.at[chunk.index, block_of(j, chunk.way)]
        return copy(spot, spot, sent.at[LIC], result_r.at[chunk.index // SECTIONS], sibling)

    def ric_copy(j, chunk):
        spot = right.at[chunk.index, xb[(0, -1, 2, 1)[j] * chunk.way]]
        return copy(spot, spot, sent.at[RIC], result_r.at[0], sibling)

    def lrs_copy(k, chunk):
        q, w = chunk.index, chunk.way
        if k == 0:
            src = own.at[yb[4], q]
        elif k == 4:
            src = own.at[yb[-3 * w], q]
        else:
            src = lrs.at[k - 1, q]
        to = on_y[w] if k < 4 else on_y[-w]
        return copy(src, lrs.at[k, q], sent.at[LRS], along_r.at[k, q], to)

    def z_copy(chunk):
        q = chunk.index
        return copy(zout.at[q], zin.at[q], sent.at[LZ], z_r.at[q], z_far)

    def lag_copy(k, chunk):
        q, w = chunk.index, chunk.way
        spot = left.at[q, yb[-k * w] if k < 4 else yb[(k - 4) * w]]
        to = on_y[w] if k < 4 else on_y[-w]
        return copy(spot, spot, sent.at[LAG], along_r.at[k, CHUNKS + q], to)

    def lag_wait(k, chunk):
        q, w = chunk.index, chunk.way
        spot = left.at[q, yb[-(k + 1) * w] if k < 4 else yb[(k - 3) * w]]
        copy(spot, spot, sent.at[LAG], along_r.at[k, CHUNKS + q], sibling).wait_recv()

    def rrs_copy(k, chunk):
        q, w = chunk.index, chunk.way
        if k == 0:
            src = rown.at[q, xb[2]]
        elif k == 1:
            src = rrs.at[0, q]
        else:
            src = rown.at[q, xb[-w]]
        to = on_x[w] if k < 2 else on_x[-w]
        return copy(src, rrs.at[k, q], sent.at[RRS], along_r.at[k, q], to)

    first_to = device(dzl=1 - 2 * first)
    second_to = device(dzl=2 * first - 1)

    def flood_copy(k, chunk):
        q = chunk.index
        spot = flood.at[k, q]
        to = first_to if k is first else second_to
        return copy(spot, spot, sent.at[RFL], along_r.at[3 + k, q], to)

    def rag_copy(k, chunk):
        q, w = chunk.index, chunk.way
        spot = right.at[q, xb[-w] if k == 1 else x]
        to = on_x[-w] if k == 2 else on_x[w]
        return copy(spot, spot, sent.at[RAG], along_r.at[5 + k, q], to)

    def rag_wait(k, chunk):
        q, w = chunk.index, chunk.way
        spot = right.at[q, xb[(-1, 2, 1)[k] * w]]
        copy(spot, spot, sent.at[RAG], along_r.at[5 + k, q], sibling).wait_recv()

    def received(part, ref):
        copy(ref, ref, sent.at[LIC], result_r.at[part], sibling).wait_recv()

    def drain(kind, ref):
        copy(ref, ref, sent.at[kind], result_r.at[0], sibling).wait_send()

    @pl.when(core == 0)
    def _():
        for d in ORDER[:3]:
            left_block(own, d)
        pl.semaphore_wait(barrier, 4)
        for d in ORDER[:3]:
            left_ship(d).wait_recv()

        def reduce_first(chunk):
            q = chunk.index
            here, there = factor(table[2, q] == 0), factor(table[2, q] == 1)
            for k, d in ((0, 4), (4, -3 * chunk.way)):
                own[yb[d], q] = own[yb[d], q] * here + sib_in[yb[d], q] * there
                lrs_copy(k, chunk).start()
        each(reduce_first)

        def begin(s):
            right_piece(ship, s)
            right_ship(s).start()
        loop(0, CHUNKS, begin)
        for d in ORDER[3:]:
            left_block(own, d)

        def merge(q, d, got):
            mine = (table[0, q] == y).astype(jnp.int32)
            here, there = factor(table[2, q] == 0, mine), factor(table[2, q] == 1, mine)
            return own[yb[d], q] * here + sib_in[yb[d], q] * there + got * factor(mine == 0)

        for h in range(1, 4):
            if h < 3:
                left_ship(3 - h).wait_recv()
                left_ship(h - 3).wait_recv()

            def reduce_next(chunk, h=h):
                q, w = chunk.index, chunk.way
                lrs_copy(h - 1, chunk).wait_recv()
                lrs[h - 1, q] = merge(q, (4 - h) * w, lrs[h - 1, q])
                lrs_copy(h, chunk).start()
                if h < 3:
                    lrs_copy(3 + h, chunk).wait_recv()
                    lrs[3 + h, q] = merge(q, -(3 - h) * w, lrs[3 + h, q])
                    lrs_copy(4 + h, chunk).start()
            each(reduce_next)
        left_ship(0).wait_recv()

        def reduce_last(chunk):
            q, w = chunk.index, chunk.way
            delta = ((table[0, q] - y) * w + Y) % Y
            near = (delta > 0).astype(jnp.int32) * (delta < 4).astype(jnp.int32)
            lrs_copy(6, chunk).wait_recv()
            lrs_copy(3, chunk).wait_recv()
            far = lrs[6, q] * factor(near == 1) + lrs[3, q] * factor(delta >= 4)
            zout[q] = merge(q, 0, far)
            z_copy(chunk).start()
        each(reduce_last)

        def gather_first(chunk):
            q = chunk.index
            root = table[1, q]
            mine, other = factor(root == zh), factor(root != zh)
            z_copy(chunk).wait_recv()
            left[q, y] = zout[q] * mine + zin[q] * other
            lag_copy(0, chunk).start()
            lag_copy(4, chunk).start()
            lic_copy(0, chunk).start()
        each(gather_first)

        for h in range(1, 5):
            def gather_next(chunk, h=h):
                lag_wait(h - 1, chunk)
                if h < 4:
                    lag_copy(h, chunk).start()
                    lag_wait(3 + h, chunk)
                    if h < 3:
                        lag_copy(4 + h, chunk).start()
                    lic_copy(4 + h, chunk).start()
                lic_copy(h, chunk).start()
            each(gather_next)

        received(0, right.at[pl.ds(CHUNKS, CHUNKS)])

    @pl.when(core == 1)
    def _():
        left_block(sib_out, ORDER[0])
        up = (zl > 0).astype(jnp.int32) + (zl < ZL - 1).astype(jnp.int32)
        pl.semaphore_wait(barrier, 3 + up)

        for i, d in enumerate(ORDER):
            if i > 0:
                left_block(sib_out, d)
            left_ship(d).start()
            if i < 2:
                continue
            for q in ((0, 1), (2, 3), (4,), (5,), (6,), (7,))[i - 2]:
                right_piece(rown, q)
                rrs_copy(0, Chunk(q, 1 - 2 * (q % 2))).start()

        def shipped(chunk):
            right_ship(chunk.index - CHUNKS).wait_recv()
            rrs_copy(0, chunk).start()
        each(shipped, CHUNKS, PIECES)

        def reduce_next(chunk):
            q, w = chunk.index, chunk.way
            root = pieces[3, q]
            mine, other = factor(root == x), factor(root != x)
            rrs_copy(0, chunk).wait_recv()
            rrs[0, q] = rown[q, xb[w]] * mine + rrs[0, q] * other
            rrs_copy(1, chunk).start()
            rrs_copy(2, chunk).start()

        def reduce_last(chunk):
            q = chunk.index
            delta = ((pieces[3, q] - x) * chunk.way + X) % X
            rrs_copy(2, chunk).wait_recv()
            rrs_copy(1, chunk).wait_recv()
            rgot[q] = pick((delta == 0, rown[q, x]), (delta == 1, rrs[2, q]), (delta >= 2, rrs[1, q]))

        def flow_first(chunk):
            q = chunk.index

            @pl.when(place == 0)
            def _():
                flood[first, q] = rgot[q]

            @pl.when(place > 0)
            def _():
                root = pieces[4, q]
                mine, other = factor(root == zl), factor(root != zl)
                flood_copy(first, chunk).wait_recv()
                flood[first, q] = rgot[q] * mine + flood[first, q] * other
            flood_copy(first, chunk).start()

        def flow_second(chunk):
            q = chunk.index
            root = pieces[4, q]
            mine, other = factor(root == zl), factor(root != zl)
            flood_copy(second, chunk).wait_recv()
            flood[second, q] = rgot[q] * mine + flood[second, q] * other

            @pl.when(place > 0)
            def _():
                flood_copy(second, chunk).start()
            right[q, x] = pick((root <= zl, flood[0, q]), (root > zl, flood[1, q]))
            rag_copy(0, chunk).start()
            rag_copy(2, chunk).start()

            @pl.when(q >= CHUNKS)
            def _():
                ric_copy(0, chunk).start()

        def gather_next(chunk):
            rag_wait(0, chunk)
            rag_copy(1, chunk).start()

            @pl.when(chunk.index >= CHUNKS)
            def _():
                ric_copy(1, chunk).start()

        def gather_last(chunk):
            rag_wait(2, chunk)
            rag_wait(1, chunk)

            @pl.when(chunk.index >= CHUNKS)
            def _():
                ric_copy(3, chunk).start()
                ric_copy(2, chunk).start()

        lag_first = 8 + 4 * place
        lag_second = 8 + 4 * (5 - place)

        def step(u):
            for parity in range(2):
                t = 2 * u + parity
                for lag, body in (
                    (0, reduce_next),
                    (8, reduce_last),
                    (lag_first, flow_first),
                    (lag_second, flow_second),
                    (lag_second + 8, gather_next),
                    (lag_second + 16, gather_last),
                ):
                    @pl.when((t >= lag) & (t < lag + PIECES))
                    def _(body=body, lag=lag, t=t, parity=parity):
                        body(Chunk(t - lag, 1 - 2 * parity))
        loop(0, (PIECES + 44) // 2, step)


    def rows_of(i):
        lhs = jnp.concatenate(
            [
                left[i // 2 * SECTIONS + s, pl.ds(i % 2 * 4, 4)].reshape(TILE, TILE)
                for s in range(SECTIONS)
            ],
            axis=1,
        )
        rhs = right[pl.ds((1 - core) * CHUNKS, CHUNKS)].reshape(SECTIONS * TILE, WIDTH)
        rows = pl.ds(pl.multiple_of(i * TILE, TILE), TILE)
        product[rows, :] = jnp.dot(lhs, rhs, preferred_element_type=jnp.float32).astype(jnp.bfloat16)
        pltpu.make_async_copy(product.at[rows], out.at[rows], out_sem).start()
    for half in range(2):
        @pl.when(core == 1)
        def _(half=half):
            received(half, left.at[pl.ds(half * SECTIONS, SECTIONS)])
        loop(2 * half, 2 * half + 2, rows_of)

    @pl.when(core == 0)
    def _():
        drain(RX, ship)
        drain(LRS, lrs)
        drain(LZ, zout)
        drain(LAG, left.at[:, pl.ds(0, 7)])
        drain(LIC, left)

    @pl.when(core == 1)
    def _():
        drain(XC, sib_out)
        drain(RRS, rrs)
        drain(RFL, flood.at[first])

        @pl.when(place > 0)
        def _():
            drain(RFL, flood.at[second])
        drain(RAG, right.at[:, pl.ds(0, 3)])
        drain(RIC, right.at[pl.ds(CHUNKS, CHUNKS)])

    pltpu.make_async_copy(product, out, out_sem).wait()


def shards(values, pattern, sections):
    bf = jnp.bfloat16
    S, C = SECTIONS, CHUNKS
    dma = pltpu.SemaphoreType.DMA
    return pl.pallas_call(
        kernel,
        name="exposure",
        out_shape=jax.ShapeDtypeStruct(values.shape, bf),
        in_specs=[
            pl.BlockSpec(memory_space=pl.ANY),
            pl.BlockSpec(memory_space=pl.ANY),
            pl.BlockSpec(memory_space=pl.ANY),
        ],
        out_specs=pl.BlockSpec(memory_space=pl.ANY),
        scratch_shapes=[
            pltpu.SMEM((S,), jnp.int32),
            pltpu.SMEM((4, 3), jnp.int32),
            pltpu.SMEM((5, C), jnp.int32),
            pltpu.SMEM((5, PIECES), jnp.int32),
            pltpu.VMEM((1024, WIDTH), bf),
            pltpu.VMEM((1024, WIDTH), bf),
            pltpu.VMEM((Y, C, LB, TILE), bf),
            pltpu.VMEM((Y, C, LB, TILE), bf),
            pltpu.VMEM((Y, C, LB, TILE), bf),
            pltpu.VMEM((7, C, LB, TILE), bf),
            pltpu.VMEM((C, LB, TILE), bf),
            pltpu.VMEM((C, LB, TILE), bf),
            pltpu.VMEM((C, Y, LB, TILE), bf),
            pltpu.VMEM((C, X, RB, WIDTH), bf),
            pltpu.VMEM((PIECES, X, RB, WIDTH), bf),
            pltpu.VMEM((3, PIECES, RB, WIDTH), bf),
            pltpu.VMEM((PIECES, RB, WIDTH), bf),
            pltpu.VMEM((2, PIECES, RB, WIDTH), bf),
            pltpu.VMEM((PIECES, X, RB, WIDTH), bf),
            dma((3,)), dma, dma((10,)), dma((2,)), dma((C,)), dma((C,)), dma((8, PIECES)),
        ],
        compiler_params=pltpu.CompilerParams(
            collective_id=0, has_side_effects=True, vmem_limit_bytes=60 << 20
        ),
        cost_estimate=pl.CostEstimate(
            flops=2 * 1024 * 1024 * 768, bytes_accessed=2 * 1024 * 768 * 2, transcendentals=0
        ),
    )(sections, pattern, values)


def solution(mesh):
    in_specs = (P("row", "col"), P("row", "col"), P())
    out_specs = P("row", "col")
    return jax.shard_map(shards, mesh=mesh, in_specs=in_specs, out_specs=out_specs, check_vma=False)
```
